768 devices in a mesh: row: 2 (over core), col: 96 (over z, y), layer: 4 (over x).
Axes of the slice: x: 4, y: 8, z: 12, core: 2. Of those that a mesh axis runs over, the one named last changes fastest.
Arguments:
- p_tiles: bfloat16 [1536, 16, 128, 128], P(('row', 'col')), may hold values from -0.8984375 to 0.8984375
- p_offs: int32 [1536, 16], replicated, may hold values from -8 to 8, as said below
- out_offs: int32 [1536, 4], P(('row', 'col')), may hold values from -16 to 16, as said below
Outputs:
- c_tiles: bfloat16 [1536, 4, 128, 128], P(('row', 'col'), 'layer')
The draws below stay inside these ranges and needn't reach their ends.
Inputs may be any that keep to these rules, and one draw needn't show every extreme that they name: `p_offs`: each row holds 16 distinct offsets. `out_offs`: each row holds 4 distinct offsets.
All inputs are finite; a program needn't handle non-finite values.
Results may differ from the reference program's by a relative error of at most 0.001.
Values may be sent and summed in bfloat16 or wider, within the bound.
No kernel may reach another device: no remote copies, remote signals or barrier semaphores. Data moves between devices by JAX's collectives and lax.ppermute only.
A program may use at most 64 MiB of HBM per device.

```python
import jax
import jax.numpy as jnp
from jax import lax

TB = 128
NZ = 16
HB = 8
NT = 1536
NZO = 4


def candidates_pick(key, count_rows, count, span):
    breadth = 2 * span + 1
    scores = jax.random.randint(key, (count_rows, breadth), 0, 1 << 20) * breadth
    scores = scores + jnp.arange(breadth, dtype=jnp.int32)[None, :]
    order = jnp.argsort(scores, axis=1)
    return (order[:, :count] - span).astype(jnp.int32)


def draw_p_offs(key, part):
    return candidates_pick(jax.random.fold_in(key, 11), NT, NZ, HB)


def draw_out_offs(key, part):
    return candidates_pick(jax.random.fold_in(key, 23), NT, NZO, 2 * HB)


def block_levels(own_key, shape, shards, least, top_value):
    gain = 1.0
    for axis_at, parts in shards:
        heights = jax.random.uniform(jax.random.fold_in(jax.random.fold_in(own_key, 6), axis_at), (parts,), jnp.float32, least / len(shards), top_value / len(shards))
        gain = gain * jnp.repeat(jnp.exp(heights), shape[axis_at] // parts).reshape((-1,) + (1,) * (len(shape) - 1 - axis_at))
    return gain


def centred(stream_key, shape, deviation, most, cuts=(), held_as=jnp.bfloat16):
    array = jax.random.normal(stream_key, shape, jnp.float32) * deviation
    if len(cuts) > 0:
        array = block_levels(stream_key, shape, cuts, -0.22, 0.18) * array
    return jnp.clip(array, min=-most, max=most).astype(held_as)


def setup_inputs(seed: int = 0) -> dict:
    seeds = jax.random.split(jax.random.key(seed), 4)
    p_tiles = centred(seeds[0], (NT, NZ, TB, TB), 0.15, 0.8984375, ((0, 192),))
    p_offs = draw_p_offs(jax.random.fold_in(seeds[3], 71), 0)
    out_offs = draw_out_offs(jax.random.fold_in(seeds[3], 71), 0)
    return dict(p_tiles=p_tiles, p_offs=p_offs, out_offs=out_offs)


def reference(p_tiles, p_offs, out_offs):
    def one_row(row):
        offsets = p_offs[row]
        targets = (row + offsets) % NT
        right_rows = p_tiles[targets].astype(jnp.float32)
        combined = offsets[:, None] + p_offs[targets]
        matches = (combined[:, :, None] == out_offs[row][None, None, :]).astype(jnp.float32)
        picked = jnp.einsum('nms,nmab->nsab', matches, right_rows)
        left_tiles = p_tiles[row].astype(jnp.float32)
        return jnp.einsum('nab,nsbc->sac', left_tiles, picked).astype(jnp.bfloat16)

    return lax.map(one_row, jnp.arange(NT, dtype=jnp.int32))
```

```python
import jax
import jax.numpy as jnp
from jax import lax
from jax.experimental import pallas as pl
from jax.experimental.pallas import tpu as pltpu
from jax.sharding import PartitionSpec as P

HB = 8
GROUP = ("row", "col")
SMEM = pltpu.SMEM
VMEM = pltpu.VMEM

BELOW = [(i, k) for i in range(8) for k in range(8) if i <= k]
ABOVE = [(i, k) for i in range(8) for k in range(8) if i >= k]


def passed_along(block, distance):
    devices = range(lax.axis_size(GROUP))
    route = [((i - distance) % len(devices), i) for i in devices]
    return lax.ppermute(block, GROUP, route)


def read_offs(p_offs, offs, sems, first):
    blocks = p_offs.shape[1] // 128
    block = first // 128
    return [
        pltpu.make_async_copy(
            p_offs.at[:, pl.ds(pl.multiple_of(lax.rem(block + part, blocks) * 128, 128), 128)],
            offs.at[part],
            sems.at[part],
        )
        for part in range(2)
    ]


def fill_table(table, offs, first, rows, nz, empty):
    start = lax.rem(first, 128)
    for r in range(rows):
        part, lane = (start + r) // 128, lax.rem(start + r, 128)
        for o in range(2 * HB + 1):
            table[r, o] = jnp.int32(empty)
        for m in range(nz):
            table[r, offs[part, m, lane] + HB] = jnp.int32(m)


def slot(table, row, offset):
    return table[row, jnp.clip(offset + HB, 0, 2 * HB)]


def send_kernel(p_offs, from_left, from_right, p_tiles, to_right, to_left, offs, table, sems):
    rows, nz = p_tiles.shape[0], p_tiles.shape[1]
    place = lax.axis_index(GROUP)
    layer = lax.axis_index("layer")
    first = place * rows
    copies = read_offs(p_offs, offs, sems, first)
    for copy in copies:
        copy.start()
    for copy in copies:
        copy.wait()
    fill_table(table, offs, first, rows, nz, 0)
    for at, (i, k) in enumerate(BELOW):
        m = slot(table, k, from_right[layer, i] - (k - rows - i))
        pltpu.make_async_copy(p_tiles.at[k, m], to_right.at[at], sems.at[2]).start()
    for at, (i, k) in enumerate(ABOVE):
        m = slot(table, k, from_left[layer, i] - (k + rows - i))
        pltpu.make_async_copy(p_tiles.at[k, m], to_left.at[at], sems.at[3]).start()
    pltpu.make_async_copy(to_right, to_right, sems.at[2]).wait()
    pltpu.make_async_copy(to_left, to_left, sems.at[3]).wait()


def own_kernel(p_offs, out_offs, p_tiles, total, left_at, offs, table, tiles, sems):
    rows, nz = p_tiles.shape[0], p_tiles.shape[1]
    whole = p_offs.shape[1]
    none = rows * nz
    place = lax.axis_index(GROUP)
    layer = lax.axis_index("layer")
    big = [
        pltpu.make_async_copy(p_tiles.at[r], tiles.at[pl.ds(r * nz, nz)], sems.at[2 + r]) for r in range(rows)
    ]
    first = lax.rem(place * rows + whole - rows, whole)
    copies = read_offs(p_offs, offs, sems, first)
    for copy in copies:
        copy.start()
    for copy in big:
        copy.start()
    tiles[none] = jnp.zeros(tiles.shape[1:], tiles.dtype)
    for copy in copies:
        copy.wait()
    fill_table(table, offs, first, 3 * rows, nz, nz)

    def left_slot(i, part, k):
        distance = k + (part - 1) * rows - i
        out = out_offs[layer, i] - distance
        m = slot(table, part * rows + k, out)
        n = slot(table, rows + i, distance)
        good = (n < nz) & (m < nz) & (out >= -HB) & (out <= HB)
        return jnp.where(good, i * nz + n, none), jnp.where(good, k * nz + m, none)

    for at, (i, k) in enumerate(BELOW):
        left_at[0, at] = left_slot(i, 0, k)[0]
    for at, (i, k) in enumerate(ABOVE):
        left_at[1, at] = left_slot(i, 2, k)[0]
    for copy in big:
        copy.wait()
    for i in range(rows):
        at = [left_slot(i, 1, k) for k in range(rows)]
        left = jnp.concatenate([tiles[a] for a, _ in at], axis=1)
        right = jnp.concatenate([tiles[b] for _, b in at], axis=0)
        total[i] = jnp.dot(left, right, preferred_element_type=jnp.float32)


def halo_kernel(left_at, p_tiles, total, below, above, out, tiles, sems):
    rows, nz = p_tiles.shape[0], p_tiles.shape[1]
    none = rows * nz
    big = [
        pltpu.make_async_copy(p_tiles.at[r], tiles.at[pl.ds(r * nz, nz)], sems.at[r]) for r in range(rows)
    ]
    for copy in big:
        copy.start()
    tiles[none] = jnp.zeros(tiles.shape[1:], tiles.dtype)
    for i in range(rows):
        big[i].wait()
        ats = [(0, at) for at, (a, _) in enumerate(BELOW) if a == i] + [(1, at) for at, (a, _) in enumerate(ABOVE) if a == i]
        left = jnp.concatenate([tiles[left_at[s, at]] for s, at in ats], axis=1)
        right = jnp.concatenate([(below, above)[s][at] for s, at in ats], axis=0)
        out[i, 0] = (total[i] + jnp.dot(left, right, preferred_element_type=jnp.float32)).astype(out.dtype)


def body(p_tiles, p_offs, out_offs):
    rows, nz, tb, _ = p_tiles.shape
    pairs = len(BELOW)
    any_spec = pl.BlockSpec(memory_space=pl.ANY)
    smem_spec = pl.BlockSpec(memory_space=SMEM)
    vmem_spec = pl.BlockSpec(memory_space=VMEM)
    limit = pltpu.CompilerParams(vmem_limit_bytes=32 << 20)
    p_offs, out_offs = p_offs.T, out_offs.T
    from_left = passed_along(out_offs, 1)
    from_right = passed_along(out_offs, -1)
    sent = jax.ShapeDtypeStruct((pairs, tb, tb), p_tiles.dtype)
    to_right, to_left = pl.pallas_call(
        send_kernel,
        out_shape=(sent, sent),
        in_specs=[any_spec, smem_spec, smem_spec, any_spec],
        out_specs=(any_spec, any_spec),
        scratch_shapes=[
            SMEM((2, nz, 128), jnp.int32),
            SMEM((rows, 2 * HB + 1), jnp.int32),
            pltpu.SemaphoreType.DMA((4,)),
        ],
        compiler_params=limit,
        name="pick_halo",
    )(p_offs, from_left, from_right, p_tiles)
    below = passed_along(to_right, 1)
    above = passed_along(to_left, -1)
    total, left_at = pl.pallas_call(
        own_kernel,
        out_shape=(
            jax.ShapeDtypeStruct((rows, tb, tb), jnp.float32),
            jax.ShapeDtypeStruct((2, pairs), jnp.int32),
        ),
        in_specs=[any_spec, smem_spec, any_spec],
        out_specs=(vmem_spec, smem_spec),
        scratch_shapes=[
            SMEM((2, nz, 128), jnp.int32),
            SMEM((3 * rows, 2 * HB + 1), jnp.int32),
            VMEM((rows * nz + 1, tb, tb), p_tiles.dtype),
            pltpu.SemaphoreType.DMA((2 + rows,)),
        ],
        compiler_params=limit,
        cost_estimate=pl.CostEstimate(flops=2 * 64 * tb**3, bytes_accessed=4 << 20, transcendentals=0),
        name="own_rows",
    )(p_offs, out_offs, p_tiles)
    return pl.pallas_call(
        halo_kernel,
        out_shape=jax.ShapeDtypeStruct((rows, 1, tb, tb), p_tiles.dtype),
        in_specs=[smem_spec, any_spec, vmem_spec, vmem_spec, vmem_spec],
        out_specs=vmem_spec,
        scratch_shapes=[
            VMEM((rows * nz + 1, tb, tb), p_tiles.dtype),
            pltpu.SemaphoreType.DMA((rows,)),
        ],
        compiler_params=limit,
        name="halo_rows",
    )(left_at, p_tiles, total, below, above)


def solution(mesh):
    return jax.shard_map(
        body,
        mesh=mesh,
        in_specs=(P(GROUP, None, None, None), P(), P(GROUP, None)),
        out_specs=P(GROUP, "layer", None, None),
        check_vma=False,
    )
```

```python
import jax
import jax.numpy as jnp
from jax import lax
from jax.experimental import pallas as pl
from jax.experimental.pallas import tpu as pltpu
from jax.sharding import PartitionSpec as P

HB = 8
WIDTH = 2 * HB + 1
GROUP = ("row", "col")
SMEM = pltpu.SMEM
VMEM = pltpu.VMEM
ANY_SPEC = pl.BlockSpec(memory_space=pl.ANY)
SMEM_SPEC = pl.BlockSpec(memory_space=SMEM)
VMEM_SPEC = pl.BlockSpec(memory_space=VMEM)
LIMIT = pltpu.CompilerParams(vmem_limit_bytes=32 << 20)

BELOW = [(i, k) for i in range(8) for k in range(8) if i <= k]
ABOVE = [(i, k) for i in range(8) for k in range(8) if i >= k]


def passed_along(block, distance):
    devices = range(lax.axis_size(GROUP))
    route = [((i - distance) % len(devices), i) for i in devices]
    return lax.ppermute(block, GROUP, route)


def slot(table, row, offset, nz):
    found = table[row, jnp.clip(offset + HB, 0, WIDTH - 1)]
    return jnp.where((offset >= -HB) & (offset <= HB), found, nz)


def fill_table(p_offs, table, offs, sems, rows, before):
    nz, whole = p_offs.shape
    first = lax.rem(lax.axis_index(GROUP) * 8 + whole - before, whole)
    block, start = first // 128, lax.rem(first, 128)
    copies = [
        pltpu.make_async_copy(
            p_offs.at[:, pl.ds(pl.multiple_of(lax.rem(block + part, whole // 128) * 128, 128), 128)],
            offs.at[part],
            sems.at[part],
        )
        for part in range(2)
    ]
    for copy in copies:
        copy.start()
    for r in range(rows):
        for o in range(WIDTH):
            table[r, o] = jnp.int32(nz)
    for copy in copies:
        copy.wait()
    for r in range(rows):
        part, lane = (start + r) // 128, lax.rem(start + r, 128)
        found = [offs[part, m, lane] + HB for m in range(nz)]
        for m in range(nz):
            table[r, found[m]] = jnp.int32(m)


def prepare_kernel(p_offs, table, offs, sems):
    fill_table(p_offs, table, offs, sems, table.shape[0], 0)


def pick_kernel(pairs, shift, table, asked, tiles, picked):
    rows, nz = tiles.shape[0], tiles.shape[1]
    layer = lax.axis_index("layer")
    for at, (i, k) in enumerate(pairs):
        m = slot(table, k, asked[layer, i] - (k - i + shift), nz)
        picked[at] = tiles[k, jnp.minimum(m, nz - 1)]


def own_kernel(p_offs, out_offs, tiles, total, left_below, left_above, table, offs, sems):
    rows, nz = tiles.shape[0], tiles.shape[1]
    fill_table(p_offs, table, offs, sems, 3 * rows, rows)
    layer = lax.axis_index("layer")

    def pair(i, k, shift):
        distance = k + shift - i
        m = slot(table, rows + shift + k, out_offs[layer, i] - distance, nz)
        n = slot(table, rows + i, distance, nz)
        left = tiles[i, jnp.minimum(n, nz - 1)]
        return jnp.where((n < nz) & (m < nz), left, jnp.zeros_like(left)), jnp.minimum(m, nz - 1)

    for left, pairs, shift in ((left_below, BELOW, -rows), (left_above, ABOVE, rows)):
        for at, (i, k) in enumerate(pairs):
            left[at] = pair(i, k, shift)[0]
    for i in range(rows):
        at = [pair(i, k, 0) for k in range(rows)]
        left = jnp.concatenate([a for a, _ in at], axis=1)
        right = jnp.concatenate([tiles[k, m] for k, (_, m) in enumerate(at)], axis=0)
        total[i] = jnp.dot(left, right, preferred_element_type=jnp.float32)


def halo_kernel(pairs, total, left, right, out):
    for i in range(total.shape[0]):
        ats = [at for at, (a, _) in enumerate(pairs) if a == i]
        product = jnp.dot(
            jnp.concatenate([left[at] for at in ats], axis=1),
            jnp.concatenate([right[at] for at in ats], axis=0),
            preferred_element_type=jnp.float32,
        )
        out[i] = (total[i] + product).astype(out.dtype)


def cost(products, moved):
    return pl.CostEstimate(flops=2 * products * 128**3, bytes_accessed=moved, transcendentals=0)


def body(p_tiles, p_offs, out_offs):
    rows, nz, tb, _ = p_tiles.shape
    count = len(BELOW)
    dtype = p_tiles.dtype
    p_offs, out_offs = p_offs.T, out_offs.T
    offs_scratch = [SMEM((2, nz, 128), jnp.int32), pltpu.SemaphoreType.DMA((2,))]
    table = pl.pallas_call(
        prepare_kernel,
        out_shape=jax.ShapeDtypeStruct((rows, WIDTH), jnp.int32),
        in_specs=[ANY_SPEC],
        out_specs=SMEM_SPEC,
        scratch_shapes=offs_scratch,
        compiler_params=LIMIT,
        cost_estimate=cost(4000, 8 << 20),
        name="prepare",
    )(p_offs)
    from_left = passed_along(out_offs, 1)
    from_right = passed_along(out_offs, -1)
    from_left, from_right = lax.optimization_barrier((from_left, from_right))

    def pick(pairs, shift, wanted, name):
        return pl.pallas_call(
            lambda *refs: pick_kernel(pairs, shift, *refs),
            out_shape=jax.ShapeDtypeStruct((count, tb, tb), dtype),
            in_specs=[SMEM_SPEC, SMEM_SPEC, VMEM_SPEC],
            out_specs=VMEM_SPEC,
            compiler_params=LIMIT,
            cost_estimate=cost(0, 2 << 20),
            name=name,
        )(table, wanted, p_tiles)

    below = passed_along(pick(BELOW, -rows, from_right, "pick_right"), 1)
    above = passed_along(pick(ABOVE, rows, from_left, "pick_left"), -1)
    left_shape = jax.ShapeDtypeStruct((count, tb, tb), dtype)
    sum_shape = jax.ShapeDtypeStruct((rows, tb, tb), jnp.float32)
    total, left_below, left_above = pl.pallas_call(
        own_kernel,
        out_shape=(sum_shape, left_shape, left_shape),
        in_specs=[ANY_SPEC, SMEM_SPEC, VMEM_SPEC],
        out_specs=(VMEM_SPEC, VMEM_SPEC, VMEM_SPEC),
        scratch_shapes=[SMEM((3 * rows, WIDTH), jnp.int32), *offs_scratch],
        compiler_params=LIMIT,
        cost_estimate=cost(64, 8 << 20),
        name="own_rows",
    )(p_offs, out_offs, p_tiles)

    def halo(pairs, total, left, right, out_shape, name):
        return pl.pallas_call(
            lambda *refs: halo_kernel(pairs, *refs),
            out_shape=out_shape,
            in_specs=[VMEM_SPEC, VMEM_SPEC, VMEM_SPEC],
            out_specs=VMEM_SPEC,
            compiler_params=LIMIT,
            cost_estimate=cost(count, 4 << 20),
            name=name,
        )(total, left, right)

    total = halo(BELOW, total, left_below, below, sum_shape, "rows_below")
    result = halo(ABOVE, total, left_above, above, jax.ShapeDtypeStruct((rows, tb, tb), dtype), "rows_above")
    return result[:, None]


def solution(mesh):
    return jax.shard_map(
        body,
        mesh=mesh,
        in_specs=(P(GROUP, None, None, None), P(), P(GROUP, None)),
        out_specs=P(GROUP, "layer", None, None),
        check_vma=False,
    )
```

```python
import jax
import jax.numpy as jnp
from jax import lax
from jax.experimental import pallas as pl
from jax.experimental.pallas import tpu as pltpu
from jax.sharding import PartitionSpec as P

HB = 8
WIDTH = 2 * HB + 1
GROUP = ("row", "col")
SMEM = pltpu.SMEM
VMEM = pltpu.VMEM
ANY_SPEC = pl.BlockSpec(memory_space=pl.ANY)
SMEM_SPEC = pl.BlockSpec(memory_space=SMEM)
VMEM_SPEC = pl.BlockSpec(memory_space=VMEM)
LIMIT = pltpu.CompilerParams(vmem_limit_bytes=32 << 20)

BELOW = [(i, k) for i in range(8) for k in range(8) if i <= k]
ABOVE = [(i, k) for i in range(8) for k in range(8) if i >= k]


def passed_along(block, distance):
    devices = range(lax.axis_size(GROUP))
    route = [((i - distance) % len(devices), i) for i in devices]
    return lax.ppermute(block, GROUP, route)


def slot(table, row, offset, nz):
    found = table[row, jnp.clip(offset + HB, 0, WIDTH - 1)]
    return jnp.where((offset >= -HB) & (offset <= HB), found, nz)


def fill_table(p_offs, table, offs, sems, rows, before):
    nz, whole = p_offs.shape
    first = lax.rem(lax.axis_index(GROUP) * 8 + whole - before, whole)
    block, start = first // 128, lax.rem(first, 128)
    copies = [
        pltpu.make_async_copy(
            p_offs.at[:, pl.ds(pl.multiple_of(lax.rem(block + part, whole // 128) * 128, 128), 128)],
            offs.at[part],
            sems.at[part],
        )
        for part in range(2)
    ]
    for copy in copies:
        copy.start()
    for r in range(rows):
        for o in range(WIDTH):
            table[r, o] = jnp.int32(nz)
    for copy in copies:
        copy.wait()
    for r in range(rows):
        part, lane = (start + r) // 128, lax.rem(start + r, 128)
        found = [offs[part, m, lane] + HB for m in range(nz)]
        for m in range(nz):
            table[r, found[m]] = jnp.int32(m)


def first_kernel(token):
    token[...] = jnp.zeros_like(token)


def pick_kernel(pairs, shift, p_offs, asked, tiles, picked, found, slots, sem):
    rows, nz = tiles.shape[0], tiles.shape[1]
    first = lax.axis_index(GROUP) * rows
    start = lax.rem(first, 128)
    offs = p_offs[:, pl.ds(pl.multiple_of(first // 128 * 128, 128), 128)]
    k = lax.broadcasted_iota(jnp.int32, offs.shape, 1) - start
    m = lax.broadcasted_iota(jnp.int32, offs.shape, 0)
    wanted = asked[pl.ds(lax.axis_index("layer"), 1), :]
    for i in range(rows):
        hit = offs == wanted[:, i : i + 1] - (k - i + shift)
        found[i : i + 1, :] = jnp.sum(jnp.where(hit, m, 0), axis=0, keepdims=True)
    copy = pltpu.make_async_copy(found, slots, sem)
    copy.start()
    copy.wait()
    for at, (i, k) in enumerate(pairs):
        picked[at] = tiles[k, slots[i, start + k]]


def own_kernel(p_offs, out_offs, tiles, token, total, left_below, left_above, table, offs, sems):
    rows, nz = tiles.shape[0], tiles.shape[1]
    fill_table(p_offs, table, offs, sems, 3 * rows, rows)
    layer = lax.axis_index("layer")

    def pair(i, k, shift):
        distance = k + shift - i
        m = slot(table, rows + shift + k, out_offs[layer, i] - distance, nz)
        n = slot(table, rows + i, distance, nz)
        left = tiles[i, jnp.minimum(n, nz - 1)]
        return jnp.where((n < nz) & (m < nz), left, jnp.zeros_like(left)), jnp.minimum(m, nz - 1)

    for left, pairs, shift in ((left_below, BELOW, -rows), (left_above, ABOVE, rows)):
        for at, (i, k) in enumerate(pairs):
            left[at] = pair(i, k, shift)[0]
    for i in range(rows):
        at = [pair(i, k, 0) for k in range(rows)]
        left = jnp.concatenate([a for a, _ in at], axis=1)
        right = jnp.concatenate([tiles[k, m] for k, (_, m) in enumerate(at)], axis=0)
        total[i] = jnp.dot(left, right, preferred_element_type=jnp.float32)


def halo_kernel(pairs, total, left, right, out):
    for i in range(total.shape[0]):
        ats = [at for at, (a, _) in enumerate(pairs) if a == i]
        product = jnp.dot(
            jnp.concatenate([left[at] for at in ats], axis=1),
            jnp.concatenate([right[at] for at in ats], axis=0),
            preferred_element_type=jnp.float32,
        )
        out[i] = (total[i] + product).astype(out.dtype)


def cost(products, moved):
    return pl.CostEstimate(flops=2 * products * 128**3, bytes_accessed=moved, transcendentals=0)


def body(p_tiles, p_offs, out_offs):
    rows, nz, tb, _ = p_tiles.shape
    count = len(BELOW)
    dtype = p_tiles.dtype
    p_offs, out_offs = p_offs.T, out_offs.T
    offs_scratch = [SMEM((2, nz, 128), jnp.int32), pltpu.SemaphoreType.DMA((2,))]
    from_left = passed_along(out_offs, 1)
    token = pl.pallas_call(
        first_kernel,
        out_shape=jax.ShapeDtypeStruct((8, 128), jnp.float32),
        out_specs=VMEM_SPEC,
        compiler_params=LIMIT,
        cost_estimate=cost(4000, 8 << 20),
        name="first",
    )()
    mine, token = lax.optimization_barrier((out_offs, token))
    from_right = passed_along(mine, -1)

    def pick(pairs, shift, wanted, name):
        return pl.pallas_call(
            lambda *refs: pick_kernel(pairs, shift, *refs),
            out_shape=jax.ShapeDtypeStruct((count, tb, tb), dtype),
            in_specs=[VMEM_SPEC, VMEM_SPEC, VMEM_SPEC],
            out_specs=VMEM_SPEC,
            scratch_shapes=[VMEM((rows, 128), jnp.int32), SMEM((rows, 128), jnp.int32), pltpu.SemaphoreType.DMA],
            compiler_params=LIMIT,
            cost_estimate=cost(0, 2 << 20),
            name=name,
        )(p_offs, wanted, p_tiles)

    for_left = pick(ABOVE, rows, from_left, "pick_left")
    from_right, for_left = lax.optimization_barrier((from_right, for_left))
    for_right = pick(BELOW, -rows, from_right, "pick_right")
    for_right, for_left = lax.optimization_barrier((for_right, for_left))
    below = passed_along(for_right, 1)
    above = passed_along(for_left, -1)
    left_shape = jax.ShapeDtypeStruct((count, tb, tb), dtype)
    sum_shape = jax.ShapeDtypeStruct((rows, tb, tb), jnp.float32)
    total, left_below, left_above = pl.pallas_call(
        own_kernel,
        out_shape=(sum_shape, left_shape, left_shape),
        in_specs=[ANY_SPEC, SMEM_SPEC, VMEM_SPEC, ANY_SPEC],
        out_specs=(VMEM_SPEC, VMEM_SPEC, VMEM_SPEC),
        scratch_shapes=[SMEM((3 * rows, WIDTH), jnp.int32), *offs_scratch],
        compiler_params=LIMIT,
        cost_estimate=cost(64, 8 << 20),
        name="own_rows",
    )(p_offs, out_offs, p_tiles, token)

    def halo(pairs, total, left, right, out_shape, name):
        return pl.pallas_call(
            lambda *refs: halo_kernel(pairs, *refs),
            out_shape=out_shape,
            in_specs=[VMEM_SPEC, VMEM_SPEC, VMEM_SPEC],
            out_specs=VMEM_SPEC,
            compiler_params=LIMIT,
            cost_estimate=cost(count, 4 << 20),
            name=name,
        )(total, left, right)

    total = halo(BELOW, total, left_below, below, sum_shape, "rows_below")
    result = halo(ABOVE, total, left_above, above, jax.ShapeDtypeStruct((rows, tb, tb), dtype), "rows_above")
    return result[:, None]


def solution(mesh):
    return jax.shard_map(
        body,
        mesh=mesh,
        in_specs=(P(GROUP, None, None, None), P(), P(GROUP, None)),
        out_specs=P(GROUP, "layer", None, None),
        check_vma=False,
    )
```
